32 devices in a mesh: rows: 8 (over z, y), cols: 4 (over x, core).
Axes of the slice: x: 2, y: 2, z: 4, core: 2. Of those that a mesh axis runs over, the one named last changes fastest.
Arguments:
- matrix: float32 [8192, 10, 512], P('rows', None, 'cols'), may hold values from -6 to 6
Outputs:
- reduced: float32 [8192, 10, 512], P('rows', None, 'cols')
- top_rows: float32 [256, 10, 512], P(None, None, 'cols')
The draws below stay inside these ranges and needn't reach their ends.
All inputs are finite; a program needn't handle non-finite values.
Results may differ from the reference program's by a relative error of at most 0.0001.
Values sent between devices are 32-bit elements; how exact they have to be, the bound alone decides.
A program may use at most 64 MiB of HBM per device.

```python
import jax
import jax.numpy as jnp
from jax import lax

BLK = 128
ROWS_DEV = 1024
ROUNDS = 10
ROWS = 8192
WIDE = 512
N_ROWS = 8


def block_scale(key, extent, pieces, least, largest):
    loudness, own = 1.0, jax.random.fold_in(key, 6)
    for axis_at, parts in pieces:
        draws = jnp.exp(jax.random.uniform(jax.random.fold_in(own, axis_at), (parts,), jnp.float32, least / len(pieces), largest / len(pieces)))
        loudness = loudness * jnp.repeat(draws, extent[axis_at] // parts).reshape([-1 if axis == axis_at else 1 for axis in range(len(extent))])
    return loudness


def noise(stream_key, dims, width, reach, cuts=(), dtype=jnp.bfloat16):
    values = jax.random.normal(stream_key, dims, jnp.float32) * width
    if len(cuts) > 0:
        values = block_scale(stream_key, dims, cuts, -0.22, 0.18) * values
    return jnp.clip(values, min=-reach, max=reach).astype(dtype)


def setup_inputs(seed: int = 0) -> dict:
    streams_of = jax.random.split(jax.random.key(seed), 2)
    matrix = noise(streams_of[0], (ROWS, ROUNDS, WIDE), 1.0, 6.0, ((0, 8), (2, 4)), jnp.float32)
    return {"matrix": matrix}


PRECISE = lax.Precision.HIGHEST

def reference(matrix):
    columns = matrix.reshape(ROWS, ROUNDS * WIDE)
    panels = columns[:, :2 * BLK]
    stacked = columns.reshape(N_ROWS, ROWS_DEV, ROUNDS * WIDE)

    def accumulate(total, slab):
        term = jnp.dot(slab[:, :2 * BLK].T.astype(jnp.float32), slab.astype(jnp.float32), precision=PRECISE, preferred_element_type=jnp.float32)
        return (total + term, None)
    cross, unused = lax.scan(accumulate, jnp.zeros((2 * BLK, ROUNDS * WIDE), jnp.float32), stacked)
    gram = cross[:, :2 * BLK]
    triangle = jnp.linalg.cholesky(gram)
    top_rows = jax.scipy.linalg.solve_triangular(triangle, cross, lower=True)
    coefficients = jax.scipy.linalg.solve_triangular(triangle, top_rows, trans=1, lower=True)
    reduced = columns - jnp.dot(panels.astype(jnp.float32), coefficients.astype(jnp.float32), precision=PRECISE, preferred_element_type=jnp.float32)
    return (reduced.reshape(ROWS, ROUNDS, WIDE), top_rows.reshape(2 * BLK, ROUNDS, WIDE))
```

```python
import functools

import jax
import jax.numpy as jnp
from jax import lax
from jax.experimental import pallas as pl
from jax.experimental.pallas import tpu as pltpu
from jax.sharding import PartitionSpec as P

PRECISE = lax.Precision.HIGHEST
MESH = pl.DeviceIdType.MESH
PIECES = 4
STRIP = 32


def product(left, right, contract):
    return lax.dot_general(
        left, right, ((contract[:1], contract[1:]), ((), ())),
        precision=PRECISE, preferred_element_type=jnp.float32)


def remote(src, dst, send, recv, row, col):
    return pltpu.make_async_remote_copy(
        src_ref=src, dst_ref=dst, send_sem=send, recv_sem=recv,
        device_id=(row, col), device_id_type=MESH)


def ring_place(index, n):
    z, y = index // 2, index % 2
    return jnp.where(y == 0, z, n - 1 - z)


def ring_row(place, n):
    place = lax.rem(place + n, n)
    return jnp.where(place < n // 2, 2 * place, 2 * (n - 1 - place) + 1)


def sums_kernel(n, chips, c_hbm, panels, total, columns, cross, slots,
                load_sem, own_sem, x_send, x_recv, d_send, d_recv, rs_send, rs_recv, ag_send, ag_recv):
    row, col = lax.axis_index("rows"), lax.axis_index("cols")
    chip, core = col // 2, col % 2
    sibling = chip * 2 + 1 - core
    place = ring_place(row, n)
    ahead, behind = ring_row(place + 1, n), ring_row(place - 1, n)
    rounds, rows_dev, blk = columns.shape
    piece = rows_dev // PIECES

    loads = [pltpu.make_async_copy(c_hbm.at[r], columns.at[r], load_sem.at[r]) for r in range(rounds)]
    for load in loads:
        load.start()

    barrier = pltpu.get_barrier_semaphore()
    for to in (ahead, behind):
        pl.semaphore_signal(barrier, inc=1, device_id=(to, col), device_id_type=MESH)
    pl.semaphore_signal(barrier, inc=1, device_id=(row, sibling), device_id_type=MESH)

    @pl.when(chip > 0)
    def _():
        pl.semaphore_signal(barrier, inc=1, device_id=(row, col - 2), device_id_type=MESH)

    @pl.when(chip < chips - 1)
    def _():
        pl.semaphore_signal(barrier, inc=1, device_id=(row, col + 2), device_id_type=MESH)

    expected = 3 + jnp.where(chip > 0, 1, 0) + jnp.where(chip < chips - 1, 1, 0)
    pl.semaphore_wait(barrier, expected)

    def part(which, at):
        return panels.at[which, pl.ds(at * piece, piece)]

    def along(at):
        return remote(part(core, at), part(core, at), x_send.at[at], x_recv.at[at], row, col + 2)

    def across(at):
        return remote(part(core, at), part(core, at), d_send.at[at], d_recv.at[at], row, sibling)

    def from_sibling(at):
        return remote(part(1 - core, at), part(1 - core, at), d_send.at[at], d_recv.at[at], row, sibling)

    @pl.when(chip == 0)
    def _():
        own = [pltpu.make_async_copy(c_hbm.at[0, pl.ds(at * piece, piece)], part(core, at), own_sem.at[at])
               for at in range(PIECES)]
        for copy in own:
            copy.start()
        for copy in own:
            copy.wait()

    for load in loads:
        load.wait()

    for at in range(PIECES):
        @pl.when(chip > 0)
        def _():
            along(at).wait_recv()

        @pl.when(chip < chips - 1)
        def _():
            along(at).start()

        across(at).start()
        from_sibling(at).wait_recv()
        rows = pl.ds(at * piece, piece)
        both = jnp.concatenate([panels[0, rows, :], panels[1, rows, :]], axis=1)
        for r in range(0, rounds + 2, 2):
            if r < rounds:
                right = jnp.concatenate([columns[r, rows, :], columns[r + 1, rows, :]], axis=1)
            else:
                right = both
            term = product(both, right, (0, 0))
            if at > 0:
                cross[r] += term[:, :blk]
                cross[r + 1] += term[:, blk:]
            else:
                cross[r] = term[:, :blk]
                cross[r + 1] = term[:, blk:]

    height = cross.shape[1] // n
    third = (rounds + 2) // 4
    chains = [(0, 1), (third, 1), (2 * third, -1), (3 * third, -1)]

    def chunk(way, back):
        at = lax.rem(place - way * back + 4 * n, n)
        return pl.ds(pl.multiple_of(at * height, height), height)

    def target(way):
        return ahead if way > 0 else behind

    sums = {}
    gathers = {}
    for step in range(n):
        for which, (first, way) in enumerate(chains):
            over = pl.ds(first, third)
            rows = chunk(way, step)
            if step > 0:
                sums[which, step - 1].wait_recv()
            if step == 0:
                source = cross.at[over, rows]
            elif step < n - 1:
                slots[step - 1, over] += cross[over, rows, :]
                source = slots.at[step - 1, over]
            else:
                total[over, rows, :] = slots[step - 1, over] + cross[over, rows, :]
            if step < n - 1:
                copy = remote(source, slots.at[step, over], rs_send.at[which, step],
                              rs_recv.at[which, step], target(way), col)
                copy.start()
                sums[which, step] = copy
    for step in range(n):
        for which, (first, way) in enumerate(chains):
            over = pl.ds(first, third)
            rows = chunk(way, step - 1)
            if step > 0:
                arrived = total.at[over, rows]
                remote(arrived, arrived, ag_send.at[which, step - 1], ag_recv.at[which, step - 1],
                       target(way), col).wait_recv()
            if step < n - 1:
                copy = remote(total.at[over, rows], total.at[over, rows], ag_send.at[which, step],
                              ag_recv.at[which, step], target(way), col)
                copy.start()
                gathers[which, step] = copy
    for copy in sums.values():
        copy.wait_send()
    for copy in gathers.values():
        copy.wait_send()
    for at in range(PIECES):
        across(at).wait_send()

        @pl.when(chip < chips - 1)
        def _():
            along(at).wait_send()


def sums(block, n, chips):
    rounds, rows_dev, blk = block.shape
    wide = 2 * blk
    shape = jax.ShapeDtypeStruct
    dma = pltpu.SemaphoreType.DMA
    vmem = pl.BlockSpec(memory_space=pltpu.VMEM)
    return pl.pallas_call(
        functools.partial(sums_kernel, n, chips),
        out_shape=(shape((2, rows_dev, blk), jnp.float32), shape((rounds + 2, wide, blk), jnp.float32)),
        in_specs=[pl.BlockSpec(memory_space=pl.ANY)],
        out_specs=(vmem, vmem),
        scratch_shapes=[
            pltpu.VMEM((rounds, rows_dev, blk), jnp.float32),
            pltpu.VMEM((rounds + 2, wide, blk), jnp.float32),
            pltpu.VMEM((n - 1, rounds + 2, wide // n, blk), jnp.float32),
            dma((rounds,)), dma((PIECES,)), dma((PIECES,)), dma((PIECES,)), dma((PIECES,)), dma((PIECES,)),
            dma((4, n - 1)), dma((4, n - 1)), dma((4, n - 1)), dma((4, n - 1)),
        ],
        compiler_params=pltpu.CompilerParams(
            collective_id=0, has_side_effects=True, vmem_limit_bytes=48 * 2**20),
        name="panel_sums",
    )(block)


def eliminate(work, inverse):
    wide = inverse.shape[0]
    for top in range(0, wide, STRIP):
        strip = work[top:top + STRIP, :]
        down = lax.broadcasted_iota(jnp.int32, (STRIP, 1), 0)
        scale = jnp.ones((STRIP, 1), jnp.float32)
        for j in range(STRIP):
            column = strip[:, top + j:top + j + 1]
            pivot = column[j:j + 1, :]
            scale = jnp.where(down == j, lax.rsqrt(pivot), scale)
            if j < STRIP - 1:
                factors = jnp.where(down > j, column * (1.0 / pivot), 0.0)
                strip = strip - factors * strip[j:j + 1, :]
        strip = strip * scale
        inverse[top:top + STRIP, :] = strip[:, wide:]
        if top + STRIP < wide:
            below = strip[:, :wide]
            work[...] -= product(below, strip, (0, 0))


def reduce_kernel(sums_ref, panels, c_ref, reduced, top_rows, work, inverse):
    rounds = sums_ref.shape[0] - 2
    blk = c_ref.shape[2]
    wide = 2 * blk
    step = pl.program_id(0)

    @pl.when(step == 0)
    def _():
        work[:, :blk] = sums_ref[rounds]
        work[:, blk:wide] = sums_ref[rounds + 1]
        across = lax.broadcasted_iota(jnp.int32, (wide, wide), 1)
        down = lax.broadcasted_iota(jnp.int32, (wide, wide), 0)
        work[:, wide:] = jnp.where(across == down, 1.0, 0.0).astype(jnp.float32)
        eliminate(work, inverse)

    cross = jnp.concatenate([sums_ref[2 * step], sums_ref[2 * step + 1]], axis=1)
    weights = product(inverse[...], cross, (1, 0))
    top_rows[0] = weights[:, :blk]
    top_rows[1] = weights[:, blk:]
    coefficients = product(inverse[...], weights, (0, 0))
    both = jnp.concatenate([panels[0], panels[1]], axis=1)
    span = product(both, coefficients, (1, 0))
    reduced[0] = c_ref[0] - span[:, :blk]
    reduced[1] = c_ref[1] - span[:, blk:]


def reduce(total, panels, block):
    rounds, rows_dev, blk = block.shape
    wide = 2 * blk
    shape = jax.ShapeDtypeStruct
    whole = lambda array: pl.BlockSpec(array.shape, lambda i: (0, 0, 0))
    pair = pl.BlockSpec((2, rows_dev, blk), lambda i: (i, 0, 0))
    return pl.pallas_call(
        reduce_kernel,
        grid=(rounds // 2,),
        out_shape=(shape(block.shape, jnp.float32), shape((rounds, wide, blk), jnp.float32)),
        in_specs=[whole(total), whole(panels), pair],
        out_specs=(pair, pl.BlockSpec((2, wide, blk), lambda i: (i, 0, 0))),
        scratch_shapes=[pltpu.VMEM((wide, 2 * wide), jnp.float32), pltpu.VMEM((wide, wide), jnp.float32)],
        compiler_params=pltpu.CompilerParams(vmem_limit_bytes=48 * 2**20),
        name="reduce_columns",
    )(total, panels, block)


def solution(mesh):
    n, chips = mesh.shape["rows"], mesh.shape["cols"] // 2

    def shards(matrix):
        block = jnp.transpose(matrix, (1, 0, 2))
        panels, total = sums(block, n, chips)
        reduced, top_rows = reduce(total, panels, block)
        return jnp.transpose(reduced, (1, 0, 2)), jnp.transpose(top_rows, (1, 0, 2))

    return jax.shard_map(
        shards,
        mesh=mesh,
        in_specs=(P("rows", None, "cols"),),
        out_specs=(P("rows", None, "cols"), P(None, None, "cols")),
        check_vma=False,
    )
```

```python
import functools

import jax
import jax.numpy as jnp
from jax import lax
from jax.experimental import pallas as pl
from jax.experimental.pallas import tpu as pltpu
from jax.sharding import PartitionSpec as P

PRECISE = lax.Precision.HIGHEST
MESH = pl.DeviceIdType.MESH
PIECES = 4
STRIP = 32


def product(left, right, contract):
    return lax.dot_general(
        left, right, ((contract[:1], contract[1:]), ((), ())),
        precision=PRECISE, preferred_element_type=jnp.float32)


def split(value):
    high = value.astype(jnp.bfloat16)
    return high, (value - high.astype(jnp.float32)).astype(jnp.bfloat16)


def split_product(left, right):
    dot = functools.partial(jnp.dot, preferred_element_type=jnp.float32)
    return dot(left[0], right[0]) + (dot(left[0], right[1]) + dot(left[1], right[0]))


def remote(src, dst, send, recv, row, col):
    return pltpu.make_async_remote_copy(
        src_ref=src, dst_ref=dst, send_sem=send, recv_sem=recv,
        device_id=(row, col), device_id_type=MESH)


def ring_place(index, n):
    z, y = index // 2, index % 2
    return jnp.where(y == 0, z, n - 1 - z)


def ring_row(place, n):
    place = lax.rem(place + n, n)
    return jnp.where(place < n // 2, 2 * place, 2 * (n - 1 - place) + 1)


def sums_kernel(n, chips, c_hbm, panels, total, inverse, columns, cross, slots, gram, inbox, mine, other, work,
                gs_send, gs_recv, gg_send, gg_recv, half_send, half_recv, load_sem, own_sem, x_send, x_recv, d_send, d_recv, rs_send, rs_recv, ag_send, ag_recv):
    row, col = lax.axis_index("rows"), lax.axis_index("cols")
    chip, core = col // 2, col % 2
    sibling = chip * 2 + 1 - core
    place = ring_place(row, n)
    ahead, behind = ring_row(place + 1, n), ring_row(place - 1, n)
    rounds, rows_dev, blk = columns.shape
    piece = rows_dev // PIECES

    loads = [pltpu.make_async_copy(c_hbm.at[r], columns.at[r], load_sem.at[r]) for r in range(rounds)]
    for load in loads:
        load.start()

    barrier = pltpu.get_barrier_semaphore()
    for far in range(1, n):
        pl.semaphore_signal(barrier, inc=1, device_id=(lax.rem(row + far, n), col), device_id_type=MESH)
    pl.semaphore_signal(barrier, inc=1, device_id=(row, sibling), device_id_type=MESH)

    @pl.when(chip > 0)
    def _():
        pl.semaphore_signal(barrier, inc=1, device_id=(row, col - 2), device_id_type=MESH)

    @pl.when(chip < chips - 1)
    def _():
        pl.semaphore_signal(barrier, inc=1, device_id=(row, col + 2), device_id_type=MESH)

    expected = n + jnp.where(chip > 0, 1, 0) + jnp.where(chip < chips - 1, 1, 0)
    pl.semaphore_wait(barrier, expected)

    def part(which, at):
        return panels.at[which, pl.ds(at * piece, piece)]

    def along(at):
        return remote(part(core, at), part(core, at), x_send.at[at], x_recv.at[at], row, col + 2)

    def across(at):
        return remote(part(core, at), part(core, at), d_send.at[at], d_recv.at[at], row, sibling)

    def from_sibling(at):
        return remote(part(1 - core, at), part(1 - core, at), d_send.at[at], d_recv.at[at], row, sibling)

    @pl.when(chip == 0)
    def _():
        own = [pltpu.make_async_copy(c_hbm.at[0, pl.ds(at * piece, piece)], part(core, at), own_sem.at[at])
               for at in range(PIECES)]
        for copy in own:
            copy.start()
        for copy in own:
            copy.wait()

    for load in loads:
        load.wait()

    owners = min(n, blk // 8)
    share = blk // owners

    def owned(owner):
        return pl.ds(pl.multiple_of(core * blk + owner * share, 8), share)

    def kept(owner):
        return pl.ds(pl.multiple_of(owner * share, 8), share)

    def only(condition, run):
        if owners == n:
            run()
        else:
            pl.when(condition)(run)

    def peer(far):
        return lax.rem(row + far, n)

    def scattered(far):
        return remote(gram.at[owned(lax.rem(peer(far), owners))], inbox.at[far - 1], gs_send.at[far - 1],
                      gs_recv.at[far - 1], peer(far), col)

    def gathered(far, owner):
        return remote(mine.at[kept(owner)], mine.at[kept(owner)], gg_send.at[far - 1],
                      gg_recv.at[far - 1], peer(far), col)

    def half(which):
        return pl.ds(pl.multiple_of(which * blk, blk), blk)

    def halved():
        return remote(mine, other, half_send.at[0], half_recv.at[0], row, sibling)

    def scatter_gram():
        for far in range(1, n):
            only(peer(far) < owners, lambda: scattered(far).start())

    def gather_gram():
        for far in range(1, n):
            only(peer(far) < owners, lambda: scattered(far).wait_send())

        def add():
            for far in range(1, n):
                scattered(far).wait_recv()
            summed = gram[owned(lax.rem(row, owners)), :]
            for far in range(1, n):
                summed = summed + inbox[far - 1]
            mine[kept(lax.rem(row, owners)), :] = summed
            for far in range(1, n):
                gathered(far, lax.rem(row, owners)).start()

        only(row < owners, add)

    def swap_gram():
        for far in range(1, n):
            sender = lax.rem(row + n - far, n)
            only(sender < owners, lambda: gathered(far, lax.rem(sender, owners)).wait_recv())
        halved().start()

    def place_gram():
        halved().wait_recv()
        across_ = lax.broadcasted_iota(jnp.int32, gram.shape, 1)
        down = lax.broadcasted_iota(jnp.int32, gram.shape, 0)
        work[half(core), :2 * blk] = mine[...]
        work[half(1 - core), :2 * blk] = other[...]
        work[:, 2 * blk:] = jnp.where(across_ == down, 1.0, 0.0).astype(jnp.float32)

    for at in range(PIECES):
        @pl.when(chip > 0)
        def _():
            along(at).wait_recv()

        @pl.when(chip < chips - 1)
        def _():
            along(at).start()

        across(at).start()
        from_sibling(at).wait_recv()
        rows = pl.ds(at * piece, piece)
        both = jnp.concatenate([panels[0, rows, :], panels[1, rows, :]], axis=1)
        term = product(both, both, (0, 0))
        gram[...] = term if at == 0 else gram[...] + term
        if at == PIECES - 1:
            scatter_gram()
        flipped = split(both.T)
        for r in range(0, rounds, 2):
            right = jnp.concatenate([columns[r, rows, :], columns[r + 1, rows, :]], axis=1)
            term = split_product(flipped, split(right))
            if at > 0:
                cross[r] += term[:, :blk]
                cross[r + 1] += term[:, blk:]
            else:
                cross[r] = term[:, :blk]
                cross[r + 1] = term[:, blk:]

    height = cross.shape[1] // n
    most, least = (rounds + 2) // 4, rounds // 2 - (rounds + 2) // 4
    chains = [(0, most, 1), (most, least, 1), (rounds // 2, most, -1), (rounds // 2 + most, least, -1)]
    items = eliminate(work, inverse)

    def chunk(way, back):
        at = lax.rem(place - way * back + 4 * n, n)
        return pl.ds(pl.multiple_of(at * height, height), height)

    def target(way):
        return ahead if way > 0 else behind

    sums = {}
    gathers = {}
    for step in range(n):
        for which, (first, count, way) in enumerate(chains):
            over = pl.ds(first, count)
            rows = chunk(way, step)
            if step > 0:
                sums[which, step - 1].wait_recv()
            if step == 0:
                source = cross.at[over, rows]
            elif step < n - 1:
                slots[step - 1, over] += cross[over, rows, :]
                source = slots.at[step - 1, over]
            else:
                total[over, rows, :] = slots[step - 1, over] + cross[over, rows, :]
            if step < n - 1:
                copy = remote(source, slots.at[step, over], rs_send.at[which, step],
                              rs_recv.at[which, step], target(way), col)
                copy.start()
                sums[which, step] = copy
            if step >= 3:
                next(items, None)
        if step == 0:
            gather_gram()
        elif step == 1:
            swap_gram()
        elif step == 2:
            place_gram()
    for step in range(n):
        for which, (first, count, way) in enumerate(chains):
            over = pl.ds(first, count)
            rows = chunk(way, step - 1)
            if step > 0:
                arrived = total.at[over, rows]
                remote(arrived, arrived, ag_send.at[which, step - 1], ag_recv.at[which, step - 1],
                       target(way), col).wait_recv()
            if step < n - 1:
                copy = remote(total.at[over, rows], total.at[over, rows], ag_send.at[which, step],
                              ag_recv.at[which, step], target(way), col)
                copy.start()
                gathers[which, step] = copy
            next(items, None)
    for item in items:
        pass
    halved().wait_send()
    only(row < owners, lambda: [gathered(far, lax.rem(row, owners)).wait_send() for far in range(1, n)] and None)
    for copy in sums.values():
        copy.wait_send()
    for copy in gathers.values():
        copy.wait_send()
    for at in range(PIECES):
        across(at).wait_send()

        @pl.when(chip < chips - 1)
        def _():
            along(at).wait_send()


def sums(block, n, chips):
    rounds, rows_dev, blk = block.shape
    wide = 2 * blk
    shape = jax.ShapeDtypeStruct
    dma = pltpu.SemaphoreType.DMA
    vmem = pl.BlockSpec(memory_space=pltpu.VMEM)
    return pl.pallas_call(
        functools.partial(sums_kernel, n, chips),
        out_shape=(shape((2, rows_dev, blk), jnp.float32), shape((rounds, wide, blk), jnp.float32),
                   shape((wide, wide), jnp.float32)),
        in_specs=[pl.BlockSpec(memory_space=pl.ANY)],
        out_specs=(vmem, vmem, vmem),
        scratch_shapes=[
            pltpu.VMEM((rounds, rows_dev, blk), jnp.float32),
            pltpu.VMEM((rounds, wide, blk), jnp.float32),
            pltpu.VMEM((n - 1, rounds, wide // n, blk), jnp.float32),
            pltpu.VMEM((wide, wide), jnp.float32),
            pltpu.VMEM((n - 1, blk // min(n, blk // 8), wide), jnp.float32),
            pltpu.VMEM((blk, wide), jnp.float32),
            pltpu.VMEM((blk, wide), jnp.float32),
            pltpu.VMEM((wide, 2 * wide), jnp.float32),
            dma((n - 1,)), dma((n - 1,)), dma((n - 1,)), dma((n - 1,)), dma((1,)), dma((1,)),
            dma((rounds,)), dma((PIECES,)), dma((PIECES,)), dma((PIECES,)), dma((PIECES,)), dma((PIECES,)),
            dma((4, n - 1)), dma((4, n - 1)), dma((4, n - 1)), dma((4, n - 1)),
        ],
        compiler_params=pltpu.CompilerParams(
            collective_id=0, has_side_effects=True, vmem_limit_bytes=48 * 2**20),
        name="panel_sums",
    )(block)


def eliminate(work, inverse):
    wide = inverse.shape[0]
    for top in range(0, wide, STRIP):
        strip = work[top:top + STRIP, :]
        down = lax.broadcasted_iota(jnp.int32, (STRIP, 1), 0)
        scale = jnp.ones((STRIP, 1), jnp.float32)
        for j in range(STRIP):
            column = strip[:, top + j:top + j + 1]
            pivot = column[j:j + 1, :]
            scale = jnp.where(down == j, lax.rsqrt(pivot), scale)
            if j < STRIP - 1:
                factors = jnp.where(down > j, column * (1.0 / pivot), 0.0)
                strip = strip - factors * strip[j:j + 1, :]
            if j % 8 == 7 and j < STRIP - 1:
                yield
        strip = strip * scale
        inverse[top:top + STRIP, :] = strip[:, wide:]
        if top + STRIP < wide:
            below = strip[:, :wide]
            work[...] -= product(below, strip, (0, 0))
        yield


def reduce_kernel(sums_ref, inverse, panels, c_ref, reduced, top_rows, high, low):
    blk = c_ref.shape[2]
    step = pl.program_id(0)

    @pl.when(step == 0)
    def _():
        high[...], low[...] = split(jnp.concatenate([panels[0], panels[1]], axis=1))

    cross = jnp.concatenate([sums_ref[2 * step], sums_ref[2 * step + 1]], axis=1)
    weights = product(inverse[...], cross, (1, 0))
    top_rows[0] = weights[:, :blk]
    top_rows[1] = weights[:, blk:]
    coefficients = product(inverse[...], weights, (0, 0))
    span = split_product((high[...], low[...]), split(coefficients))
    reduced[0] = c_ref[0] - span[:, :blk]
    reduced[1] = c_ref[1] - span[:, blk:]


def reduce(total, inverse, panels, block):
    rounds, rows_dev, blk = block.shape
    wide = 2 * blk
    shape = jax.ShapeDtypeStruct
    whole = lambda array: pl.BlockSpec(array.shape, lambda i: (0,) * len(array.shape))
    pair = pl.BlockSpec((2, rows_dev, blk), lambda i: (i, 0, 0))
    return pl.pallas_call(
        reduce_kernel,
        grid=(rounds // 2,),
        out_shape=(shape(block.shape, jnp.float32), shape((rounds, wide, blk), jnp.float32)),
        in_specs=[whole(total), whole(inverse), whole(panels), pair],
        out_specs=(pair, pl.BlockSpec((2, wide, blk), lambda i: (i, 0, 0))),
        scratch_shapes=[pltpu.VMEM((rows_dev, wide), jnp.bfloat16)] * 2,
        compiler_params=pltpu.CompilerParams(vmem_limit_bytes=48 * 2**20),
        name="reduce_columns",
    )(total, inverse, panels, block)


def solution(mesh):
    n, chips = mesh.shape["rows"], mesh.shape["cols"] // 2

    def shards(matrix):
        block = jnp.transpose(matrix, (1, 0, 2))
        panels, total, inverse = sums(block, n, chips)
        reduced, top_rows = reduce(total, inverse, panels, block)
        return jnp.transpose(reduced, (1, 0, 2)), jnp.transpose(top_rows, (1, 0, 2))

    return jax.shard_map(
        shards,
        mesh=mesh,
        in_specs=(P("rows", None, "cols"),),
        out_specs=(P("rows", None, "cols"), P(None, None, "cols")),
        check_vma=False,
    )
```

```python
import functools

import jax
import jax.numpy as jnp
from jax import lax
from jax.experimental import pallas as pl
from jax.experimental.pallas import tpu as pltpu
from jax.sharding import PartitionSpec as P

PRECISE = lax.Precision.HIGHEST
MESH = pl.DeviceIdType.MESH
PIECES = 4
STRIP = 32


def product(left, right, contract):
    return lax.dot_general(
        left, right, ((contract[:1], contract[1:]), ((), ())),
        precision=PRECISE, preferred_element_type=jnp.float32)


def split(value):
    high = value.astype(jnp.bfloat16)
    return high, (value - high.astype(jnp.float32)).astype(jnp.bfloat16)


def split_product(left, right):
    dot = functools.partial(jnp.dot, preferred_element_type=jnp.float32)
    return dot(left[0], right[0]) + (dot(left[0], right[1]) + dot(left[1], right[0]))


def remote(src, dst, send, recv, row, col):
    return pltpu.make_async_remote_copy(
        src_ref=src, dst_ref=dst, send_sem=send, recv_sem=recv,
        device_id=(row, col), device_id_type=MESH)


def sums_kernel(n, chips, c_hbm, panels, total, inverse, columns, cross, slots, gram, inbox, mine, other, work,
                gs_send, gs_recv, gg_send, gg_recv, half_send, half_recv, load_sem, own_sem, x_send, x_recv, d_send, d_recv, rs_send, rs_recv, ag_send, ag_recv):
    row, col = lax.axis_index("rows"), lax.axis_index("cols")
    chip, core = col // 2, col % 2
    sibling = chip * 2 + 1 - core
    rounds, rows_dev, blk = columns.shape
    piece = rows_dev // PIECES

    loads = [pltpu.make_async_copy(c_hbm.at[r], columns.at[r], load_sem.at[r]) for r in range(rounds)]
    for load in loads:
        load.start()

    barrier = pltpu.get_barrier_semaphore()
    for far in range(1, n):
        pl.semaphore_signal(barrier, inc=1, device_id=(lax.rem(row + far, n), col), device_id_type=MESH)
    pl.semaphore_signal(barrier, inc=1, device_id=(row, sibling), device_id_type=MESH)

    @pl.when(chip > 0)
    def _():
        pl.semaphore_signal(barrier, inc=1, device_id=(row, col - 2), device_id_type=MESH)

    @pl.when(chip < chips - 1)
    def _():
        pl.semaphore_signal(barrier, inc=1, device_id=(row, col + 2), device_id_type=MESH)

    expected = n + jnp.where(chip > 0, 1, 0) + jnp.where(chip < chips - 1, 1, 0)
    pl.semaphore_wait(barrier, expected)

    def part(which, at):
        return panels.at[which, pl.ds(at * piece, piece)]

    def along(at):
        return remote(part(core, at), part(core, at), x_send.at[at], x_recv.at[at], row, col + 2)

    def across(at):
        return remote(part(core, at), part(core, at), d_send.at[at], d_recv.at[at], row, sibling)

    def from_sibling(at):
        return remote(part(1 - core, at), part(1 - core, at), d_send.at[at], d_recv.at[at], row, sibling)

    @pl.when(chip == 0)
    def _():
        own = [pltpu.make_async_copy(c_hbm.at[0, pl.ds(at * piece, piece)], part(core, at), own_sem.at[at])
               for at in range(PIECES)]
        for copy in own:
            copy.start()
        for copy in own:
            copy.wait()

    for load in loads:
        load.wait()

    owners = min(n, blk // 8)
    share = blk // owners

    def owned(owner):
        return pl.ds(pl.multiple_of(core * blk + owner * share, 8), share)

    def kept(owner):
        return pl.ds(pl.multiple_of(owner * share, 8), share)

    def only(condition, run):
        if owners == n:
            run()
        else:
            pl.when(condition)(run)

    def peer(far):
        return lax.rem(row + far, n)

    def scattered(far):
        return remote(gram.at[owned(lax.rem(peer(far), owners))], inbox.at[far - 1], gs_send.at[far - 1],
                      gs_recv.at[far - 1], peer(far), col)

    def gathered(far, owner):
        return remote(mine.at[kept(owner)], mine.at[kept(owner)], gg_send.at[far - 1],
                      gg_recv.at[far - 1], peer(far), col)

    def half(which):
        return pl.ds(pl.multiple_of(which * blk, blk), blk)

    def halved():
        return remote(mine, other, half_send.at[0], half_recv.at[0], row, sibling)

    def scatter_gram():
        for far in range(1, n):
            only(peer(far) < owners, lambda: scattered(far).start())

    def gather_gram():
        for far in range(1, n):
            only(peer(far) < owners, lambda: scattered(far).wait_send())

        def add():
            for far in range(1, n):
                scattered(far).wait_recv()
            summed = gram[owned(lax.rem(row, owners)), :]
            for far in range(1, n):
                summed = summed + inbox[far - 1]
            mine[kept(lax.rem(row, owners)), :] = summed
            for far in range(1, n):
                gathered(far, lax.rem(row, owners)).start()

        only(row < owners, add)

    def swap_gram():
        for far in range(1, n):
            sender = lax.rem(row + n - far, n)
            only(sender < owners, lambda: gathered(far, lax.rem(sender, owners)).wait_recv())
        halved().start()

    def place_gram():
        halved().wait_recv()
        across_ = lax.broadcasted_iota(jnp.int32, gram.shape, 1)
        down = lax.broadcasted_iota(jnp.int32, gram.shape, 0)
        work[half(core), :2 * blk] = mine[...]
        work[half(1 - core), :2 * blk] = other[...]
        work[:, 2 * blk:] = jnp.where(across_ == down, 1.0, 0.0).astype(jnp.float32)

    for at in range(PIECES):
        @pl.when(chip > 0)
        def _():
            along(at).wait_recv()

        @pl.when(chip < chips - 1)
        def _():
            along(at).start()

        across(at).start()
        from_sibling(at).wait_recv()
        rows = pl.ds(at * piece, piece)
        both = jnp.concatenate([panels[0, rows, :], panels[1, rows, :]], axis=1)
        term = product(both, both, (0, 0))
        gram[...] = term if at == 0 else gram[...] + term
        if at == PIECES - 1:
            scatter_gram()
        flipped = split(both.T)
        for r in range(0, rounds, 2):
            right = jnp.concatenate([columns[r, rows, :], columns[r + 1, rows, :]], axis=1)
            term = split_product(flipped, split(right))
            if at > 0:
                cross[r] += term[:, :blk]
                cross[r + 1] += term[:, blk:]
            else:
                cross[r] = term[:, :blk]
                cross[r + 1] = term[:, blk:]

    wide = 2 * blk
    bits = n.bit_length() - 1
    plain = list(range(bits))
    swapped = [1, 0] + plain[2:] if bits > 1 else plain
    chains = [(first, plain if first % 4 == 0 else swapped) for first in range(0, rounds, 2)]
    items = eliminate(work, inverse)

    def side(bit):
        return (row // 2 ** bit) % 2

    def partner(bit):
        return row + (1 - 2 * side(bit)) * 2 ** bit

    def start_of(order, phases):
        at = 0
        for t in range(phases):
            at = at + side(order[t]) * (wide >> (t + 1))
        return at

    def span_of(at, size):
        return pl.ds(pl.multiple_of(at, 8), size)

    def halve(which, t):
        first, order = chains[which]
        over, size = pl.ds(first, 2), wide >> (t + 1)
        sent = start_of(order, t) + (1 - side(order[t])) * size
        return remote(cross.at[over, span_of(sent, size)], slots.at[over, pl.ds(wide - 2 * size, size)],
                      rs_send.at[which, t], rs_recv.at[which, t], partner(order[t]), col)

    def double(which, t):
        first, order = chains[which]
        size = wide >> (t + 1)
        held = total.at[pl.ds(first, 2), span_of(start_of(order, t + 1), size)]
        return remote(held, held, ag_send.at[which, t], ag_recv.at[which, t], partner(order[t]), col)

    def add(which, t):
        first, order = chains[which]
        over, size = pl.ds(first, 2), wide >> (t + 1)
        kept_rows = span_of(start_of(order, t + 1), size)
        into = total if t == bits - 1 else cross
        into[over, kept_rows, :] = cross[over, kept_rows, :] + slots[over, pl.ds(wide - 2 * size, size), :]

    early = [gather_gram, swap_gram, place_gram]
    for which in range(len(chains)):
        halve(which, 0).start()
    for t in range(2 * bits):
        for which in range(len(chains)):
            if early:
                early.pop(0)()
            else:
                next(items, None)
            if t < bits:
                halve(which, t).wait_recv()
                add(which, t)
            else:
                double(which, 2 * bits - 1 - t).wait_recv()
            if t < bits - 1:
                halve(which, t + 1).start()
            elif t < 2 * bits - 1:
                double(which, 2 * bits - 2 - t).start()
    for item in items:
        pass
    halved().wait_send()
    only(row < owners, lambda: [gathered(far, lax.rem(row, owners)).wait_send() for far in range(1, n)] and None)
    for which in range(len(chains)):
        for t in range(bits):
            halve(which, t).wait_send()
            double(which, t).wait_send()
    for at in range(PIECES):
        across(at).wait_send()

        @pl.when(chip < chips - 1)
        def _():
            along(at).wait_send()


def sums(block, n, chips):
    rounds, rows_dev, blk = block.shape
    wide = 2 * blk
    shape = jax.ShapeDtypeStruct
    dma = pltpu.SemaphoreType.DMA
    vmem = pl.BlockSpec(memory_space=pltpu.VMEM)
    return pl.pallas_call(
        functools.partial(sums_kernel, n, chips),
        out_shape=(shape((2, rows_dev, blk), jnp.float32), shape((rounds, wide, blk), jnp.float32),
                   shape((wide, wide), jnp.float32)),
        in_specs=[pl.BlockSpec(memory_space=pl.ANY)],
        out_specs=(vmem, vmem, vmem),
        scratch_shapes=[
            pltpu.VMEM((rounds, rows_dev, blk), jnp.float32),
            pltpu.VMEM((rounds, wide, blk), jnp.float32),
            pltpu.VMEM((rounds, wide - wide // n, blk), jnp.float32),
            pltpu.VMEM((wide, wide), jnp.float32),
            pltpu.VMEM((n - 1, blk // min(n, blk // 8), wide), jnp.float32),
            pltpu.VMEM((blk, wide), jnp.float32),
            pltpu.VMEM((blk, wide), jnp.float32),
            pltpu.VMEM((wide, 2 * wide), jnp.float32),
            dma((n - 1,)), dma((n - 1,)), dma((n - 1,)), dma((n - 1,)), dma((1,)), dma((1,)),
            dma((rounds,)), dma((PIECES,)), dma((PIECES,)), dma((PIECES,)), dma((PIECES,)), dma((PIECES,)),
            *[dma((rounds // 2, n.bit_length() - 1))] * 4,
        ],
        compiler_params=pltpu.CompilerParams(
            collective_id=0, has_side_effects=True, vmem_limit_bytes=48 * 2**20),
        name="panel_sums",
    )(block)


def eliminate(work, inverse):
    wide = inverse.shape[0]
    lanes = wide // 2
    down = lax.broadcasted_iota(jnp.int32, (STRIP, lanes), 0)
    inverse[:lanes, lanes:] = jnp.zeros((lanes, lanes), jnp.float32)
    for top in range(0, wide, STRIP):
        low = top // lanes
        live = slice(low * lanes, low * lanes + 3 * lanes)
        strip = work[top:top + STRIP, live]
        scale = jnp.ones((STRIP, lanes), jnp.float32)
        lane = top - low * lanes
        for j in range(0, STRIP, 2):
            first = jnp.broadcast_to(strip[:, lane + j:lane + j + 1], (STRIP, lanes))
            second = jnp.broadcast_to(strip[:, lane + j + 1:lane + j + 2], (STRIP, lanes))
            pivot = first[j:j + 1, :]
            outer = jnp.where(down > j, first * (1.0 / pivot), 0.0)
            second = second - outer * second[j:j + 1, :]
            next_pivot = second[j + 1:j + 2, :]
            inner = jnp.where(down > j + 1, second * (1.0 / next_pivot), 0.0)
            scale = jnp.where(down == j, lax.rsqrt(pivot), scale)
            scale = jnp.where(down == j + 1, lax.rsqrt(next_pivot), scale)
            upper = strip[j:j + 1, :]
            lower = strip[j + 1:j + 2, :] - jnp.concatenate([outer[j + 1:j + 2, :]] * 3, axis=1) * upper
            strip = strip - (jnp.concatenate([outer] * 3, axis=1) * upper
                             + jnp.concatenate([inner] * 3, axis=1) * lower)
            if j % 8 == 6 and j < STRIP - 2:
                yield
        strip = strip * jnp.concatenate([scale] * 3, axis=1)
        if low == 0:
            inverse[top:top + STRIP, :lanes] = strip[:, 2 * lanes:]
        else:
            inverse[top:top + STRIP, :] = strip[:, lanes:]
        if top + STRIP < wide:
            above = (top + STRIP) // lanes * lanes
            below = strip[:, above - low * lanes:wide - low * lanes]
            work[above:, live] -= product(below, strip, (0, 0))
        yield


def reduce_kernel(sums_ref, inverse, panels, c_ref, reduced, top_rows, high, low):
    blk = c_ref.shape[2]
    step = pl.program_id(0)

    @pl.when(step == 0)
    def _():
        high[...], low[...] = split(jnp.concatenate([panels[0], panels[1]], axis=1))

    cross = jnp.concatenate([sums_ref[2 * step], sums_ref[2 * step + 1]], axis=1)
    weights = product(inverse[...], cross, (1, 0))
    top_rows[0] = weights[:, :blk]
    top_rows[1] = weights[:, blk:]
    coefficients = product(inverse[...], weights, (0, 0))
    span = split_product((high[...], low[...]), split(coefficients))
    reduced[0] = c_ref[0] - span[:, :blk]
    reduced[1] = c_ref[1] - span[:, blk:]


def reduce(total, inverse, panels, block):
    rounds, rows_dev, blk = block.shape
    wide = 2 * blk
    shape = jax.ShapeDtypeStruct
    whole = lambda array: pl.BlockSpec(array.shape, lambda i: (0,) * len(array.shape))
    pair = pl.BlockSpec((2, rows_dev, blk), lambda i: (i, 0, 0))
    return pl.pallas_call(
        reduce_kernel,
        grid=(rounds // 2,),
        out_shape=(shape(block.shape, jnp.float32), shape((rounds, wide, blk), jnp.float32)),
        in_specs=[whole(total), whole(inverse), whole(panels), pair],
        out_specs=(pair, pl.BlockSpec((2, wide, blk), lambda i: (i, 0, 0))),
        scratch_shapes=[pltpu.VMEM((rows_dev, wide), jnp.bfloat16)] * 2,
        compiler_params=pltpu.CompilerParams(vmem_limit_bytes=48 * 2**20),
        name="reduce_columns",
    )(total, inverse, panels, block)


def solution(mesh):
    n, chips = mesh.shape["rows"], mesh.shape["cols"] // 2

    def shards(matrix):
        block = jnp.transpose(matrix, (1, 0, 2))
        panels, total, inverse = sums(block, n, chips)
        reduced, top_rows = reduce(total, inverse, panels, block)
        return jnp.transpose(reduced, (1, 0, 2)), jnp.transpose(top_rows, (1, 0, 2))

    return jax.shard_map(
        shards,
        mesh=mesh,
        in_specs=(P("rows", None, "cols"),),
        out_specs=(P("rows", None, "cols"), P(None, None, "cols")),
        check_vma=False,
    )
```

```python
import functools

import jax
import jax.numpy as jnp
from jax import lax
from jax.experimental import pallas as pl
from jax.experimental.pallas import tpu as pltpu
from jax.sharding import PartitionSpec as P

PRECISE = lax.Precision.HIGHEST
MESH = pl.DeviceIdType.MESH
PIECES = 4
STRIP = 32


def product(left, right, contract):
    return lax.dot_general(
        left, right, ((contract[:1], contract[1:]), ((), ())),
        precision=PRECISE, preferred_element_type=jnp.float32)


def split(value):
    high = value.astype(jnp.bfloat16)
    return high, (value - high.astype(jnp.float32)).astype(jnp.bfloat16)


def split_product(left, right):
    dot = functools.partial(jnp.dot, preferred_element_type=jnp.float32)
    return dot(left[0], right[0]) + (dot(left[0], right[1]) + dot(left[1], right[0]))


def remote(src, dst, send, recv, row, col):
    return pltpu.make_async_remote_copy(
        src_ref=src, dst_ref=dst, send_sem=send, recv_sem=recv,
        device_id=(row, col), device_id_type=MESH)


def sums_kernel(n, chips, c_hbm, panels, total, inverse, columns, cross, slots, gram, inbox, mine, other, work,
                gs_send, gs_recv, gg_send, gg_recv, half_send, half_recv, load_sem, own_sem, x_send, x_recv, d_send, d_recv, rs_send, rs_recv, ag_send, ag_recv):
    row, col = lax.axis_index("rows"), lax.axis_index("cols")
    chip, core = col // 2, col % 2
    sibling = chip * 2 + 1 - core
    rounds, rows_dev, blk = columns.shape
    piece = rows_dev // PIECES

    barrier = pltpu.get_barrier_semaphore()
    for far in range(1, n):
        pl.semaphore_signal(barrier, inc=1, device_id=(lax.rem(row + far, n), col), device_id_type=MESH)
    pl.semaphore_signal(barrier, inc=1, device_id=(row, sibling), device_id_type=MESH)

    @pl.when(chip > 0)
    def _():
        pl.semaphore_signal(barrier, inc=1, device_id=(row, col - 2), device_id_type=MESH)

    @pl.when(chip < chips - 1)
    def _():
        pl.semaphore_signal(barrier, inc=1, device_id=(row, col + 2), device_id_type=MESH)

    expected = n + jnp.where(chip > 0, 1, 0) + jnp.where(chip < chips - 1, 1, 0)
    pl.semaphore_wait(barrier, expected)

    def part(which, at):
        return panels.at[which, pl.ds(at * piece, piece)]

    def along(at):
        return remote(part(core, at), part(core, at), x_send.at[at], x_recv.at[at], row, col + 2)

    def across(at):
        return remote(part(core, at), part(core, at), d_send.at[at], d_recv.at[at], row, sibling)

    def from_sibling(at):
        return remote(part(1 - core, at), part(1 - core, at), d_send.at[at], d_recv.at[at], row, sibling)

    @pl.when(chip == 0)
    def _():
        own = [pltpu.make_async_copy(c_hbm.at[0, pl.ds(at * piece, piece)], part(core, at), own_sem.at[at])
               for at in range(PIECES)]
        for copy in own:
            copy.start()
        for at in range(PIECES):
            own[at].wait()
            if chips > 1:
                along(at).start()
            across(at).start()

    loads = [pltpu.make_async_copy(c_hbm.at[r], columns.at[r], load_sem.at[r]) for r in range(rounds)]
    for load in loads:
        load.start()

    owners = min(n, blk // 8)
    share = blk // owners

    def owned(owner):
        return pl.ds(pl.multiple_of(core * blk + owner * share, 8), share)

    def kept(owner):
        return pl.ds(pl.multiple_of(owner * share, 8), share)

    def only(condition, run):
        if owners == n:
            run()
        else:
            pl.when(condition)(run)

    def peer(far):
        return lax.rem(row + far, n)

    def scattered(far):
        return remote(gram.at[owned(lax.rem(peer(far), owners))], inbox.at[far - 1], gs_send.at[far - 1],
                      gs_recv.at[far - 1], peer(far), col)

    def gathered(far, owner):
        return remote(mine.at[kept(owner)], mine.at[kept(owner)], gg_send.at[far - 1],
                      gg_recv.at[far - 1], peer(far), col)

    def half(which):
        return pl.ds(pl.multiple_of(which * blk, blk), blk)

    def halved():
        return remote(mine, other, half_send.at[0], half_recv.at[0], row, sibling)

    def scatter_gram():
        for far in range(1, n):
            only(peer(far) < owners, lambda: scattered(far).start())

    def gather_gram():
        for far in range(1, n):
            only(peer(far) < owners, lambda: scattered(far).wait_send())

        def add():
            for far in range(1, n):
                scattered(far).wait_recv()
            summed = gram[owned(lax.rem(row, owners)), :]
            for far in range(1, n):
                summed = summed + inbox[far - 1]
            mine[kept(lax.rem(row, owners)), :] = summed
            for far in range(1, n):
                gathered(far, lax.rem(row, owners)).start()

        only(row < owners, add)

    def swap_gram():
        for far in range(1, n):
            sender = lax.rem(row + n - far, n)
            only(sender < owners, lambda: gathered(far, lax.rem(sender, owners)).wait_recv())
        halved().start()

    def place_gram():
        halved().wait_recv()
        across_ = lax.broadcasted_iota(jnp.int32, gram.shape, 1)
        down = lax.broadcasted_iota(jnp.int32, gram.shape, 0)
        work[half(core), :2 * blk] = mine[...]
        work[half(1 - core), :2 * blk] = other[...]
        work[:, 2 * blk:] = jnp.where(across_ == down, 1.0, 0.0).astype(jnp.float32)

    wide = 2 * blk
    bits = n.bit_length() - 1
    plain = list(range(bits))
    swapped = [1, 0] + plain[2:] if bits > 1 else plain
    chains = [(first, swapped if first == 2 else plain) for first in range(0, rounds, 2)]
    items = eliminate(work, inverse)

    def side(bit):
        return (row // 2 ** bit) % 2

    def partner(bit):
        return row + (1 - 2 * side(bit)) * 2 ** bit

    def start_of(order, phases):
        at = 0
        for t in range(phases):
            at = at + side(order[t]) * (wide >> (t + 1))
        return at

    def span_of(at, size):
        return pl.ds(pl.multiple_of(at, 8), size)

    def halve(which, t):
        first, order = chains[which]
        over, size = pl.ds(first, 2), wide >> (t + 1)
        sent = start_of(order, t) + (1 - side(order[t])) * size
        return remote(cross.at[over, span_of(sent, size)], slots.at[over, pl.ds(wide - 2 * size, size)],
                      rs_send.at[which, t], rs_recv.at[which, t], partner(order[t]), col)

    def double(which, t):
        first, order = chains[which]
        size = wide >> (t + 1)
        held = total.at[pl.ds(first, 2), span_of(start_of(order, t + 1), size)]
        return remote(held, held, ag_send.at[which, t], ag_recv.at[which, t], partner(order[t]), col)

    def add(which, t):
        first, order = chains[which]
        over, size = pl.ds(first, 2), wide >> (t + 1)
        kept_rows = span_of(start_of(order, t + 1), size)
        into = total if t == bits - 1 else cross
        into[over, kept_rows, :] = cross[over, kept_rows, :] + slots[over, pl.ds(wide - 2 * size, size), :]

    for at in range(PIECES):
        @pl.when(chip > 0)
        def _():
            along(at).wait_recv()

            @pl.when(chip < chips - 1)
            def _():
                along(at).start()

            across(at).start()

        if at == 0:
            for load in loads:
                load.wait()
        from_sibling(at).wait_recv()
        rows = pl.ds(at * piece, piece)
        both = jnp.concatenate([panels[0, rows, :], panels[1, rows, :]], axis=1)
        term = product(both, both, (0, 0))
        gram[...] = term if at == 0 else gram[...] + term
        if at == PIECES - 1:
            scatter_gram()
        flipped = split(both.T)
        for r in range(0, rounds, 2):
            right = jnp.concatenate([columns[r, rows, :], columns[r + 1, rows, :]], axis=1)
            term = split_product(flipped, split(right))
            if at > 0:
                cross[r] += term[:, :blk]
                cross[r + 1] += term[:, blk:]
            else:
                cross[r] = term[:, :blk]
                cross[r + 1] = term[:, blk:]
            if at == PIECES - 1:
                halve(r // 2, 0).start()

    early = [gather_gram, swap_gram, place_gram]
    for t in range(2 * bits):
        for which in range(len(chains)):
            if early:
                early.pop(0)()
            else:
                next(items, None)
                if which == 0:
                    next(items, None)
            if t < bits:
                halve(which, t).wait_recv()
                add(which, t)
            else:
                double(which, 2 * bits - 1 - t).wait_recv()
            if t < bits - 1:
                halve(which, t + 1).start()
            elif t < 2 * bits - 1:
                double(which, 2 * bits - 2 - t).start()
    for item in items:
        pass
    halved().wait_send()
    only(row < owners, lambda: [gathered(far, lax.rem(row, owners)).wait_send() for far in range(1, n)] and None)
    for which in range(len(chains)):
        for t in range(bits):
            halve(which, t).wait_send()
            double(which, t).wait_send()
    for at in range(PIECES):
        across(at).wait_send()

        @pl.when(chip < chips - 1)
        def _():
            along(at).wait_send()


def sums(block, n, chips):
    rounds, rows_dev, blk = block.shape
    wide = 2 * blk
    shape = jax.ShapeDtypeStruct
    dma = pltpu.SemaphoreType.DMA
    vmem = pl.BlockSpec(memory_space=pltpu.VMEM)
    return pl.pallas_call(
        functools.partial(sums_kernel, n, chips),
        out_shape=(shape((2, rows_dev, blk), jnp.float32), shape((rounds, wide, blk), jnp.float32),
                   shape((wide, wide), jnp.float32)),
        in_specs=[pl.BlockSpec(memory_space=pl.ANY)],
        out_specs=(vmem, vmem, vmem),
        scratch_shapes=[
            pltpu.VMEM((rounds, rows_dev, blk), jnp.float32),
            pltpu.VMEM((rounds, wide, blk), jnp.float32),
            pltpu.VMEM((rounds, wide - wide // n, blk), jnp.float32),
            pltpu.VMEM((wide, wide), jnp.float32),
            pltpu.VMEM((n - 1, blk // min(n, blk // 8), wide), jnp.float32),
            pltpu.VMEM((blk, wide), jnp.float32),
            pltpu.VMEM((blk, wide), jnp.float32),
            pltpu.VMEM((wide, 2 * wide), jnp.float32),
            dma((n - 1,)), dma((n - 1,)), dma((n - 1,)), dma((n - 1,)), dma((1,)), dma((1,)),
            dma((rounds,)), dma((PIECES,)), dma((PIECES,)), dma((PIECES,)), dma((PIECES,)), dma((PIECES,)),
            *[dma((rounds // 2, n.bit_length() - 1))] * 4,
        ],
        compiler_params=pltpu.CompilerParams(
            collective_id=0, has_side_effects=True, vmem_limit_bytes=48 * 2**20),
        name="panel_sums",
    )(block)


def eliminate(work, inverse):
    wide = inverse.shape[0]
    lanes = wide // 2
    down = lax.broadcasted_iota(jnp.int32, (STRIP, lanes), 0)
    inverse[:lanes, lanes:] = jnp.zeros((lanes, lanes), jnp.float32)
    for top in range(0, wide, STRIP):
        low = top // lanes
        live = slice(low * lanes, low * lanes + 3 * lanes)
        strip = work[top:top + STRIP, live]
        scale = jnp.ones((STRIP, lanes), jnp.float32)
        lane = top - low * lanes
        for j in range(0, STRIP, 2):
            first = jnp.broadcast_to(strip[:, lane + j:lane + j + 1], (STRIP, lanes))
            second = jnp.broadcast_to(strip[:, lane + j + 1:lane + j + 2], (STRIP, lanes))
            pivot = first[j:j + 1, :]
            outer = jnp.where(down > j, first * (1.0 / pivot), 0.0)
            second = second - outer * second[j:j + 1, :]
            next_pivot = second[j + 1:j + 2, :]
            inner = jnp.where(down > j + 1, second * (1.0 / next_pivot), 0.0)
            scale = jnp.where(down == j, lax.rsqrt(pivot), scale)
            scale = jnp.where(down == j + 1, lax.rsqrt(next_pivot), scale)
            upper = strip[j:j + 1, :]
            lower = strip[j + 1:j + 2, :] - jnp.concatenate([outer[j + 1:j + 2, :]] * 3, axis=1) * upper
            strip = strip - (jnp.concatenate([outer] * 3, axis=1) * upper
                             + jnp.concatenate([inner] * 3, axis=1) * lower)
            if j % 8 == 6 and j < STRIP - 2:
                yield
        strip = strip * jnp.concatenate([scale] * 3, axis=1)
        if low == 0:
            inverse[top:top + STRIP, :lanes] = strip[:, 2 * lanes:]
        else:
            inverse[top:top + STRIP, :] = strip[:, lanes:]
        if top + STRIP < wide:
            above = (top + STRIP) // lanes * lanes
            below = strip[:, above - low * lanes:wide - low * lanes]
            work[above:, live] -= product(below, strip, (0, 0))
        yield


def reduce_kernel(sums_ref, inverse, panels, c_ref, reduced, top_rows, high, low, forward, backward):
    blk = c_ref.shape[2]
    step = pl.program_id(0)

    @pl.when(step == 0)
    def _():
        forward[0], forward[1] = split(inverse[...])
        backward[0], backward[1] = split(inverse[...].T)
        high[...], low[...] = split(jnp.concatenate([panels[0], panels[1]], axis=1))

    cross = jnp.concatenate([sums_ref[2 * step], sums_ref[2 * step + 1]], axis=1)
    weights = split_product((forward[0], forward[1]), split(cross))
    top_rows[0] = weights[:, :blk]
    top_rows[1] = weights[:, blk:]
    coefficients = split_product((backward[0], backward[1]), split(weights))
    span = split_product((high[...], low[...]), split(coefficients))
    reduced[0] = c_ref[0] - span[:, :blk]
    reduced[1] = c_ref[1] - span[:, blk:]


def reduce(total, inverse, panels, block):
    rounds, rows_dev, blk = block.shape
    wide = 2 * blk
    shape = jax.ShapeDtypeStruct
    whole = lambda array: pl.BlockSpec(array.shape, lambda i: (0,) * len(array.shape))
    pair = pl.BlockSpec((2, rows_dev, blk), lambda i: (i, 0, 0))
    return pl.pallas_call(
        reduce_kernel,
        grid=(rounds // 2,),
        out_shape=(shape(block.shape, jnp.float32), shape((rounds, wide, blk), jnp.float32)),
        in_specs=[whole(total), whole(inverse), whole(panels), pair],
        out_specs=(pair, pl.BlockSpec((2, wide, blk), lambda i: (i, 0, 0))),
        scratch_shapes=[pltpu.VMEM((rows_dev, wide), jnp.bfloat16)] * 2 + [pltpu.VMEM((2, wide, wide), jnp.bfloat16)] * 2,
        compiler_params=pltpu.CompilerParams(vmem_limit_bytes=48 * 2**20),
        name="reduce_columns",
    )(total, inverse, panels, block)


def solution(mesh):
    n, chips = mesh.shape["rows"], mesh.shape["cols"] // 2

    def shards(matrix):
        block = jnp.transpose(matrix, (1, 0, 2))
        panels, total, inverse = sums(block, n, chips)
        reduced, top_rows = reduce(total, inverse, panels, block)
        return jnp.transpose(reduced, (1, 0, 2)), jnp.transpose(top_rows, (1, 0, 2))

    return jax.shard_map(
        shards,
        mesh=mesh,
        in_specs=(P("rows", None, "cols"),),
        out_specs=(P("rows", None, "cols"), P(None, None, "cols")),
        check_vma=False,
    )
```

```python
import functools

import jax
import jax.numpy as jnp
from jax import lax
from jax.experimental import pallas as pl
from jax.experimental.pallas import tpu as pltpu
from jax.sharding import PartitionSpec as P

PRECISE = lax.Precision.HIGHEST
MESH = pl.DeviceIdType.MESH
PIECES = 4
STRIP = 32


def product(left, right, contract):
    return lax.dot_general(
        left, right, ((contract[:1], contract[1:]), ((), ())),
        precision=PRECISE, preferred_element_type=jnp.float32)


def split(value):
    high = value.astype(jnp.bfloat16)
    return high, (value - high.astype(jnp.float32)).astype(jnp.bfloat16)


def split_product(left, right):
    deep_left = jnp.concatenate([left[0], left[0], left[1]], axis=1)
    deep_right = jnp.concatenate([right[1], right[0], right[0]], axis=0)
    return jnp.dot(deep_left, deep_right, preferred_element_type=jnp.float32)


def remote(src, dst, send, recv, row, col):
    return pltpu.make_async_remote_copy(
        src_ref=src, dst_ref=dst, send_sem=send, recv_sem=recv,
        device_id=(row, col), device_id_type=MESH)


def sums_kernel(n, chips, c_hbm, panels, total, inverse, columns, cross, slots, gram, inbox, mine, other, work,
                gs_send, gs_recv, gg_send, gg_recv, half_send, half_recv, load_sem, own_sem, x_send, x_recv, d_send, d_recv, rs_send, rs_recv, ag_send, ag_recv):
    row, col = lax.axis_index("rows"), lax.axis_index("cols")
    chip, core = col // 2, col % 2
    sibling = chip * 2 + 1 - core
    rounds, rows_dev, blk = columns.shape
    piece = rows_dev // PIECES

    barrier = pltpu.get_barrier_semaphore()
    for far in range(1, n):
        pl.semaphore_signal(barrier, inc=1, device_id=(lax.rem(row + far, n), col), device_id_type=MESH)
    pl.semaphore_signal(barrier, inc=1, device_id=(row, sibling), device_id_type=MESH)

    @pl.when(chip > 0)
    def _():
        pl.semaphore_signal(barrier, inc=1, device_id=(row, col - 2), device_id_type=MESH)

    @pl.when(chip < chips - 1)
    def _():
        pl.semaphore_signal(barrier, inc=1, device_id=(row, col + 2), device_id_type=MESH)

    expected = n + jnp.where(chip > 0, 1, 0) + jnp.where(chip < chips - 1, 1, 0)
    pl.semaphore_wait(barrier, expected)

    def part(which, at):
        return panels.at[which, pl.ds(at * piece, piece)]

    def along(at):
        return remote(part(core, at), part(core, at), x_send.at[at], x_recv.at[at], row, col + 2)

    def across(at):
        return remote(part(core, at), part(core, at), d_send.at[at], d_recv.at[at], row, sibling)

    def from_sibling(at):
        return remote(part(1 - core, at), part(1 - core, at), d_send.at[at], d_recv.at[at], row, sibling)

    @pl.when(chip == 0)
    def _():
        own = [pltpu.make_async_copy(c_hbm.at[0, pl.ds(at * piece, piece)], part(core, at), own_sem.at[at])
               for at in range(PIECES)]
        for copy in own:
            copy.start()
        for at in range(PIECES):
            own[at].wait()
            if chips > 1:
                along(at).start()
            across(at).start()

    loads = [pltpu.make_async_copy(c_hbm.at[r], columns.at[r], load_sem.at[r]) for r in range(rounds)]
    for load in loads:
        load.start()

    owners = min(n, blk // 8)
    share = blk // owners

    def owned(owner):
        return pl.ds(pl.multiple_of(core * blk + owner * share, 8), share)

    def kept(owner):
        return pl.ds(pl.multiple_of(owner * share, 8), share)

    def only(condition, run):
        if owners == n:
            run()
        else:
            pl.when(condition)(run)

    def peer(far):
        return lax.rem(row + far, n)

    def scattered(far):
        return remote(gram.at[owned(lax.rem(peer(far), owners))], inbox.at[far - 1], gs_send.at[far - 1],
                      gs_recv.at[far - 1], peer(far), col)

    def gathered(far, owner):
        return remote(mine.at[kept(owner)], mine.at[kept(owner)], gg_send.at[far - 1],
                      gg_recv.at[far - 1], peer(far), col)

    def half(which):
        return pl.ds(pl.multiple_of(which * blk, blk), blk)

    def halved():
        return remote(mine, other, half_send.at[0], half_recv.at[0], row, sibling)

    def scatter_gram():
        for far in range(1, n):
            only(peer(far) < owners, lambda: scattered(far).start())

    def gather_gram():
        for far in range(1, n):
            only(peer(far) < owners, lambda: scattered(far).wait_send())

        def add():
            for far in range(1, n):
                scattered(far).wait_recv()
            summed = gram[owned(lax.rem(row, owners)), :]
            for far in range(1, n):
                summed = summed + inbox[far - 1]
            mine[kept(lax.rem(row, owners)), :] = summed
            for far in range(1, n):
                gathered(far, lax.rem(row, owners)).start()

        only(row < owners, add)

    def swap_gram():
        for far in range(1, n):
            sender = lax.rem(row + n - far, n)
            only(sender < owners, lambda: gathered(far, lax.rem(sender, owners)).wait_recv())
        halved().start()

    def place_gram():
        halved().wait_recv()
        across_ = lax.broadcasted_iota(jnp.int32, gram.shape, 1)
        down = lax.broadcasted_iota(jnp.int32, gram.shape, 0)
        work[half(core), :2 * blk] = mine[...]
        work[half(1 - core), :2 * blk] = other[...]
        work[:, 2 * blk:] = jnp.where(across_ == down, 1.0, 0.0).astype(jnp.float32)

    wide = 2 * blk
    bits = n.bit_length() - 1
    plain = list(range(bits))
    swapped = [1, 0] + plain[2:] if bits > 1 else plain
    chains = [(first, plain if first % 4 == 0 else swapped) for first in range(0, rounds, 2)]
    items = eliminate(work, inverse)

    def side(bit):
        return (row // 2 ** bit) % 2

    def partner(bit):
        return row + (1 - 2 * side(bit)) * 2 ** bit

    def start_of(order, phases):
        at = 0
        for t in range(phases):
            at = at + side(order[t]) * (wide >> (t + 1))
        return at

    def span_of(at, size):
        return pl.ds(pl.multiple_of(at, 8), size)

    def halve(which, t):
        first, order = chains[which]
        over, size = pl.ds(first, 2), wide >> (t + 1)
        sent = start_of(order, t) + (1 - side(order[t])) * size
        return remote(cross.at[over, span_of(sent, size)], slots.at[over, pl.ds(wide - 2 * size, size)],
                      rs_send.at[which, t], rs_recv.at[which, t], partner(order[t]), col)

    def double(which, t):
        first, order = chains[which]
        size = wide >> (t + 1)
        held = total.at[pl.ds(first, 2), span_of(start_of(order, t + 1), size)]
        return remote(held, held, ag_send.at[which, t], ag_recv.at[which, t], partner(order[t]), col)

    def add(which, t):
        first, order = chains[which]
        over, size = pl.ds(first, 2), wide >> (t + 1)
        kept_rows = span_of(start_of(order, t + 1), size)
        into = total if t == bits - 1 else cross
        into[over, kept_rows, :] = cross[over, kept_rows, :] + slots[over, pl.ds(wide - 2 * size, size), :]

    for at in range(PIECES):
        @pl.when(chip > 0)
        def _():
            along(at).wait_recv()

            @pl.when(chip < chips - 1)
            def _():
                along(at).start()

            across(at).start()

        if at == 0:
            for load in loads:
                load.wait()
        from_sibling(at).wait_recv()
        rows = pl.ds(at * piece, piece)
        both = jnp.concatenate([panels[0, rows, :], panels[1, rows, :]], axis=1)
        term = product(both, both, (0, 0))
        gram[...] = term if at == 0 else gram[...] + term
        if at == PIECES - 1:
            scatter_gram()
        flipped = split(both.T)
        for r in range(0, rounds, 2):
            right = jnp.concatenate([columns[r, rows, :], columns[r + 1, rows, :]], axis=1)
            term = split_product(flipped, split(right))
            if at > 0:
                cross[r] += term[:, :blk]
                cross[r + 1] += term[:, blk:]
            else:
                cross[r] = term[:, :blk]
                cross[r + 1] = term[:, blk:]
            if at == PIECES - 1:
                halve(r // 2, 0).start()

    early = [gather_gram, swap_gram, place_gram]
    for t in range(2 * bits):
        for which in range(len(chains)):
            if early:
                early.pop(0)()
            else:
                next(items, None)
            if t < bits:
                halve(which, t).wait_recv()
                add(which, t)
            else:
                double(which, 2 * bits - 1 - t).wait_recv()
            if t < bits - 1:
                halve(which, t + 1).start()
            elif t < 2 * bits - 1:
                double(which, 2 * bits - 2 - t).start()
    for item in items:
        pass
    halved().wait_send()
    only(row < owners, lambda: [gathered(far, lax.rem(row, owners)).wait_send() for far in range(1, n)] and None)
    for which in range(len(chains)):
        for t in range(bits):
            halve(which, t).wait_send()
            double(which, t).wait_send()
    for at in range(PIECES):
        across(at).wait_send()

        @pl.when(chip < chips - 1)
        def _():
            along(at).wait_send()


def sums(block, n, chips):
    rounds, rows_dev, blk = block.shape
    wide = 2 * blk
    shape = jax.ShapeDtypeStruct
    dma = pltpu.SemaphoreType.DMA
    vmem = pl.BlockSpec(memory_space=pltpu.VMEM)
    return pl.pallas_call(
        functools.partial(sums_kernel, n, chips),
        out_shape=(shape((2, rows_dev, blk), jnp.float32), shape((rounds, wide, blk), jnp.float32),
                   shape((wide, wide), jnp.float32)),
        in_specs=[pl.BlockSpec(memory_space=pl.ANY)],
        out_specs=(vmem, vmem, vmem),
        scratch_shapes=[
            pltpu.VMEM((rounds, rows_dev, blk), jnp.float32),
            pltpu.VMEM((rounds, wide, blk), jnp.float32),
            pltpu.VMEM((rounds, wide - wide // n, blk), jnp.float32),
            pltpu.VMEM((wide, wide), jnp.float32),
            pltpu.VMEM((n - 1, blk // min(n, blk // 8), wide), jnp.float32),
            pltpu.VMEM((blk, wide), jnp.float32),
            pltpu.VMEM((blk, wide), jnp.float32),
            pltpu.VMEM((wide, 2 * wide), jnp.float32),
            dma((n - 1,)), dma((n - 1,)), dma((n - 1,)), dma((n - 1,)), dma((1,)), dma((1,)),
            dma((rounds,)), dma((PIECES,)), dma((PIECES,)), dma((PIECES,)), dma((PIECES,)), dma((PIECES,)),
            *[dma((rounds // 2, n.bit_length() - 1))] * 4,
        ],
        compiler_params=pltpu.CompilerParams(
            collective_id=0, has_side_effects=True, vmem_limit_bytes=48 * 2**20),
        name="panel_sums",
    )(block)


def eliminate(work, inverse):
    wide = inverse.shape[0]
    lanes = wide // 2
    down = lax.broadcasted_iota(jnp.int32, (STRIP, lanes), 0)
    inverse[:lanes, lanes:] = jnp.zeros((lanes, lanes), jnp.float32)
    for top in range(0, wide, STRIP):
        low = top // lanes
        live = slice(low * lanes, low * lanes + 3 * lanes)
        strip = work[top:top + STRIP, live]
        scale = jnp.ones((STRIP, lanes), jnp.float32)
        lane = top - low * lanes
        for j in range(0, STRIP, 2):
            first = jnp.broadcast_to(strip[:, lane + j:lane + j + 1], (STRIP, lanes))
            second = jnp.broadcast_to(strip[:, lane + j + 1:lane + j + 2], (STRIP, lanes))
            pivot = first[j:j + 1, :]
            outer = jnp.where(down > j, first * (1.0 / pivot), 0.0)
            second = second - outer * second[j:j + 1, :]
            next_pivot = second[j + 1:j + 2, :]
            inner = jnp.where(down > j + 1, second * (1.0 / next_pivot), 0.0)
            scale = jnp.where(down == j, lax.rsqrt(pivot), scale)
            scale = jnp.where(down == j + 1, lax.rsqrt(next_pivot), scale)
            upper = strip[j:j + 1, :]
            lower = strip[j + 1:j + 2, :] - jnp.concatenate([outer[j + 1:j + 2, :]] * 3, axis=1) * upper
            strip = strip - (jnp.concatenate([outer] * 3, axis=1) * upper
                             + jnp.concatenate([inner] * 3, axis=1) * lower)
            if j % 8 == 6 and j < STRIP - 2:
                yield
        strip = strip * jnp.concatenate([scale] * 3, axis=1)
        if low == 0:
            inverse[top:top + STRIP, :lanes] = strip[:, 2 * lanes:]
        else:
            inverse[top:top + STRIP, :] = strip[:, lanes:]
        if top + STRIP < wide:
            above = (top + STRIP) // lanes * lanes
            below = strip[:, above - low * lanes:wide - low * lanes]
            work[above:, live] -= product(below, strip, (0, 0))
        yield


def reduce_kernel(sums_ref, inverse, panels, c_ref, reduced, top_rows, high, low, forward, backward):
    blk = c_ref.shape[2]
    step = pl.program_id(0)

    @pl.when(step == 0)
    def _():
        forward[0], forward[1] = split(inverse[...])
        backward[0], backward[1] = split(inverse[...].T)
        high[...], low[...] = split(jnp.concatenate([panels[0], panels[1]], axis=1))

    cross = jnp.concatenate([sums_ref[2 * step], sums_ref[2 * step + 1]], axis=1)
    weights = split_product((forward[0], forward[1]), split(cross))
    top_rows[0] = weights[:, :blk]
    top_rows[1] = weights[:, blk:]
    coefficients = split_product((backward[0], backward[1]), split(weights))
    span = split_product((high[...], low[...]), split(coefficients))
    reduced[0] = c_ref[0] - span[:, :blk]
    reduced[1] = c_ref[1] - span[:, blk:]


def reduce(total, inverse, panels, block):
    rounds, rows_dev, blk = block.shape
    wide = 2 * blk
    shape = jax.ShapeDtypeStruct
    whole = lambda array: pl.BlockSpec(array.shape, lambda i: (0,) * len(array.shape))
    pair = pl.BlockSpec((2, rows_dev, blk), lambda i: (i, 0, 0))
    return pl.pallas_call(
        reduce_kernel,
        grid=(rounds // 2,),
        out_shape=(shape(block.shape, jnp.float32), shape((rounds, wide, blk), jnp.float32)),
        in_specs=[whole(total), whole(inverse), whole(panels), pair],
        out_specs=(pair, pl.BlockSpec((2, wide, blk), lambda i: (i, 0, 0))),
        scratch_shapes=[pltpu.VMEM((rows_dev, wide), jnp.bfloat16)] * 2 + [pltpu.VMEM((2, wide, wide), jnp.bfloat16)] * 2,
        compiler_params=pltpu.CompilerParams(vmem_limit_bytes=48 * 2**20),
        name="reduce_columns",
    )(total, inverse, panels, block)


def solution(mesh):
    n, chips = mesh.shape["rows"], mesh.shape["cols"] // 2

    def shards(matrix):
        block = jnp.transpose(matrix, (1, 0, 2))
        panels, total, inverse = sums(block, n, chips)
        reduced, top_rows = reduce(total, inverse, panels, block)
        return jnp.transpose(reduced, (1, 0, 2)), jnp.transpose(top_rows, (1, 0, 2))

    return jax.shard_map(
        shards,
        mesh=mesh,
        in_specs=(P("rows", None, "cols"),),
        out_specs=(P("rows", None, "cols"), P(None, None, "cols")),
        check_vma=False,
    )
```

```python
import functools

import jax
import jax.numpy as jnp
from jax import lax
from jax.experimental import pallas as pl
from jax.experimental.pallas import tpu as pltpu
from jax.sharding import PartitionSpec as P

PRECISE = lax.Precision.HIGHEST
MESH = pl.DeviceIdType.MESH
PIECES = 4
STRIP = 32


def product(left, right, contract):
    return lax.dot_general(
        left, right, ((contract[:1], contract[1:]), ((), ())),
        precision=PRECISE, preferred_element_type=jnp.float32)


def split(value):
    high = value.astype(jnp.bfloat16)
    return high, (value - high.astype(jnp.float32)).astype(jnp.bfloat16)


def split_product(left, right):
    deep_left = jnp.concatenate([left[0], left[0], left[1]], axis=1)
    deep_right = jnp.concatenate([right[1], right[0], right[0]], axis=0)
    return jnp.dot(deep_left, deep_right, preferred_element_type=jnp.float32)


def remote(src, dst, send, recv, row, col):
    return pltpu.make_async_remote_copy(
        src_ref=src, dst_ref=dst, send_sem=send, recv_sem=recv,
        device_id=(row, col), device_id_type=MESH)


def sums_kernel(n, chips, c_hbm, panels, total, inverse, columns, cross, slots, gram, inbox, mine, other, work,
                gs_send, gs_recv, gg_send, gg_recv, half_send, half_recv, load_sem, own_sem, x_send, x_recv, d_send, d_recv, rs_send, rs_recv, ag_send, ag_recv):
    row, col = lax.axis_index("rows"), lax.axis_index("cols")
    chip, core = col // 2, col % 2
    sibling = chip * 2 + 1 - core
    rounds, rows_dev, blk = columns.shape
    piece = rows_dev // PIECES

    barrier = pltpu.get_barrier_semaphore()
    for far in range(1, n):
        pl.semaphore_signal(barrier, inc=1, device_id=(lax.rem(row + far, n), col), device_id_type=MESH)
    pl.semaphore_signal(barrier, inc=1, device_id=(row, sibling), device_id_type=MESH)

    @pl.when(chip > 0)
    def _():
        pl.semaphore_signal(barrier, inc=1, device_id=(row, col - 2), device_id_type=MESH)

    @pl.when(chip < chips - 1)
    def _():
        pl.semaphore_signal(barrier, inc=1, device_id=(row, col + 2), device_id_type=MESH)

    expected = n + jnp.where(chip > 0, 1, 0) + jnp.where(chip < chips - 1, 1, 0)
    pl.semaphore_wait(barrier, expected)

    def part(which, at):
        return panels.at[which, pl.ds(at * piece, piece)]

    def along(at):
        return remote(part(core, at), part(core, at), x_send.at[at], x_recv.at[at], row, col + 2)

    def across(at):
        return remote(part(core, at), part(core, at), d_send.at[at], d_recv.at[at], row, sibling)

    def from_sibling(at):
        return remote(part(1 - core, at), part(1 - core, at), d_send.at[at], d_recv.at[at], row, sibling)

    @pl.when(chip == 0)
    def _():
        own = [pltpu.make_async_copy(c_hbm.at[0, pl.ds(at * piece, piece)], part(core, at), own_sem.at[at])
               for at in range(PIECES)]
        for copy in own:
            copy.start()
        for at in range(PIECES):
            own[at].wait()
            if chips > 1:
                along(at).start()
            across(at).start()

    loads = [pltpu.make_async_copy(c_hbm.at[r], columns.at[r], load_sem.at[r]) for r in range(rounds)]
    for load in loads:
        load.start()

    owners = min(n, blk // 8)
    share = blk // owners

    def owned(owner):
        return pl.ds(pl.multiple_of(core * blk + owner * share, 8), share)

    def kept(owner):
        return pl.ds(pl.multiple_of(owner * share, 8), share)

    def only(condition, run):
        if owners == n:
            run()
        else:
            pl.when(condition)(run)

    def peer(far):
        return lax.rem(row + far, n)

    def scattered(far):
        return remote(gram.at[owned(lax.rem(peer(far), owners))], inbox.at[far - 1], gs_send.at[far - 1],
                      gs_recv.at[far - 1], peer(far), col)

    def gathered(far, owner):
        return remote(mine.at[kept(owner)], mine.at[kept(owner)], gg_send.at[far - 1],
                      gg_recv.at[far - 1], peer(far), col)

    def half(which):
        return pl.ds(pl.multiple_of(which * blk, blk), blk)

    def halved():
        return remote(mine, other, half_send.at[0], half_recv.at[0], row, sibling)

    def scatter_gram():
        for far in range(1, n):
            only(peer(far) < owners, lambda: scattered(far).start())

    def gather_gram():
        for far in range(1, n):
            only(peer(far) < owners, lambda: scattered(far).wait_send())

        def add():
            for far in range(1, n):
                scattered(far).wait_recv()
            summed = gram[owned(lax.rem(row, owners)), :]
            for far in range(1, n):
                summed = summed + inbox[far - 1]
            mine[kept(lax.rem(row, owners)), :] = summed
            for far in range(1, n):
                gathered(far, lax.rem(row, owners)).start()

        only(row < owners, add)

    def swap_gram():
        for far in range(1, n):
            sender = lax.rem(row + n - far, n)
            only(sender < owners, lambda: gathered(far, lax.rem(sender, owners)).wait_recv())
        halved().start()

    def place_gram():
        halved().wait_recv()
        across_ = lax.broadcasted_iota(jnp.int32, gram.shape, 1)
        down = lax.broadcasted_iota(jnp.int32, gram.shape, 0)
        work[half(core), :2 * blk] = mine[...]
        work[half(1 - core), :2 * blk] = other[...]
        work[:, 2 * blk:] = jnp.where(across_ == down, 1.0, 0.0).astype(jnp.float32)

    wide = 2 * blk
    bits = n.bit_length() - 1
    plain = list(range(bits))
    swapped = [1, 0] + plain[2:] if bits > 1 else plain
    chains = [(first, plain if first % 4 == 2 else swapped) for first in range(0, rounds, 2)]
    items = eliminate(work, inverse)

    def side(bit):
        return (row // 2 ** bit) % 2

    def partner(bit):
        return row + (1 - 2 * side(bit)) * 2 ** bit

    def start_of(order, phases):
        at = 0
        for t in range(phases):
            at = at + side(order[t]) * (wide >> (t + 1))
        return at

    def span_of(at, size):
        return pl.ds(pl.multiple_of(at, 8), size)

    def halve(which, t):
        first, order = chains[which]
        over, size = pl.ds(first, 2), wide >> (t + 1)
        sent = start_of(order, t) + (1 - side(order[t])) * size
        return remote(cross.at[over, span_of(sent, size)], slots.at[over, pl.ds(wide - 2 * size, size)],
                      rs_send.at[which, t], rs_recv.at[which, t], partner(order[t]), col)

    def double(which, t):
        first, order = chains[which]
        size = wide >> (t + 1)
        held = total.at[pl.ds(first, 2), span_of(start_of(order, t + 1), size)]
        return remote(held, held, ag_send.at[which, t], ag_recv.at[which, t], partner(order[t]), col)

    def add(which, t):
        first, order = chains[which]
        over, size = pl.ds(first, 2), wide >> (t + 1)
        kept_rows = span_of(start_of(order, t + 1), size)
        into = total if t == bits - 1 else cross
        into[over, kept_rows, :] = cross[over, kept_rows, :] + slots[over, pl.ds(wide - 2 * size, size), :]

    for at in range(PIECES):
        @pl.when(chip > 0)
        def _():
            along(at).wait_recv()

            @pl.when(chip < chips - 1)
            def _():
                along(at).start()

            across(at).start()

        if at == 0:
            for load in loads:
                load.wait()
        from_sibling(at).wait_recv()
        rows = pl.ds(at * piece, piece)
        both = jnp.concatenate([panels[0, rows, :], panels[1, rows, :]], axis=1)
        term = product(both, both, (0, 0))
        gram[...] = term if at == 0 else gram[...] + term
        if at == PIECES - 1:
            scatter_gram()
        flipped = split(both.T)
        for r in range(0, rounds, 2):
            right = jnp.concatenate([columns[r, rows, :], columns[r + 1, rows, :]], axis=1)
            term = split_product(flipped, split(right))
            if at > 0:
                cross[r] += term[:, :blk]
                cross[r + 1] += term[:, blk:]
            else:
                cross[r] = term[:, :blk]
                cross[r + 1] = term[:, blk:]
            if at == PIECES - 1:
                halve(r // 2, 0).start()

    early = [gather_gram, swap_gram, place_gram]
    for t in range(2 * bits):
        for which in range(len(chains)):
            if early:
                early.pop(0)()
            else:
                next(items, None)
            if t < bits:
                halve(which, t).wait_recv()
                add(which, t)
            else:
                double(which, 2 * bits - 1 - t).wait_recv()
            if t < bits - 1:
                halve(which, t + 1).start()
            elif t < 2 * bits - 1:
                double(which, 2 * bits - 2 - t).start()
    for item in items:
        pass
    halved().wait_send()
    only(row < owners, lambda: [gathered(far, lax.rem(row, owners)).wait_send() for far in range(1, n)] and None)
    for which in range(len(chains)):
        for t in range(bits):
            halve(which, t).wait_send()
            double(which, t).wait_send()
    for at in range(PIECES):
        across(at).wait_send()

        @pl.when(chip < chips - 1)
        def _():
            along(at).wait_send()


def sums(block, n, chips):
    rounds, rows_dev, blk = block.shape
    wide = 2 * blk
    shape = jax.ShapeDtypeStruct
    dma = pltpu.SemaphoreType.DMA
    vmem = pl.BlockSpec(memory_space=pltpu.VMEM)
    return pl.pallas_call(
        functools.partial(sums_kernel, n, chips),
        out_shape=(shape((2, rows_dev, blk), jnp.float32), shape((rounds, wide, blk), jnp.float32),
                   shape((wide, wide), jnp.float32)),
        in_specs=[pl.BlockSpec(memory_space=pl.ANY)],
        out_specs=(vmem, vmem, vmem),
        scratch_shapes=[
            pltpu.VMEM((rounds, rows_dev, blk), jnp.float32),
            pltpu.VMEM((rounds, wide, blk), jnp.float32),
            pltpu.VMEM((rounds, wide - wide // n, blk), jnp.float32),
            pltpu.VMEM((wide, wide), jnp.float32),
            pltpu.VMEM((n - 1, blk // min(n, blk // 8), wide), jnp.float32),
            pltpu.VMEM((blk, wide), jnp.float32),
            pltpu.VMEM((blk, wide), jnp.float32),
            pltpu.VMEM((wide, 2 * wide), jnp.float32),
            dma((n - 1,)), dma((n - 1,)), dma((n - 1,)), dma((n - 1,)), dma((1,)), dma((1,)),
            dma((rounds,)), dma((PIECES,)), dma((PIECES,)), dma((PIECES,)), dma((PIECES,)), dma((PIECES,)),
            *[dma((rounds // 2, n.bit_length() - 1))] * 4,
        ],
        compiler_params=pltpu.CompilerParams(
            collective_id=0, has_side_effects=True, vmem_limit_bytes=48 * 2**20),
        name="panel_sums",
    )(block)


def eliminate(work, inverse):
    wide = inverse.shape[0]
    lanes = wide // 2
    down = lax.broadcasted_iota(jnp.int32, (STRIP, lanes), 0)
    inverse[:lanes, lanes:] = jnp.zeros((lanes, lanes), jnp.float32)
    for top in range(0, wide, STRIP):
        low = top // lanes
        live = slice(low * lanes, low * lanes + 3 * lanes)
        strip = work[top:top + STRIP, live]
        scale = jnp.ones((STRIP, lanes), jnp.float32)
        lane = top - low * lanes
        for j in range(0, STRIP, 2):
            first = jnp.broadcast_to(strip[:, lane + j:lane + j + 1], (STRIP, lanes))
            second = jnp.broadcast_to(strip[:, lane + j + 1:lane + j + 2], (STRIP, lanes))
            pivot = first[j:j + 1, :]
            outer = jnp.where(down > j, first * (1.0 / pivot), 0.0)
            second = second - outer * second[j:j + 1, :]
            next_pivot = second[j + 1:j + 2, :]
            inner = jnp.where(down > j + 1, second * (1.0 / next_pivot), 0.0)
            scale = jnp.where(down == j, lax.rsqrt(pivot), scale)
            scale = jnp.where(down == j + 1, lax.rsqrt(next_pivot), scale)
            upper = strip[j:j + 1, :]
            lower = strip[j + 1:j + 2, :] - jnp.concatenate([outer[j + 1:j + 2, :]] * 3, axis=1) * upper
            strip = strip - (jnp.concatenate([outer] * 3, axis=1) * upper
                             + jnp.concatenate([inner] * 3, axis=1) * lower)
            if j % 8 == 6 and j < STRIP - 2:
                yield
        strip = strip * jnp.concatenate([scale] * 3, axis=1)
        if low == 0:
            inverse[top:top + STRIP, :lanes] = strip[:, 2 * lanes:]
        else:
            inverse[top:top + STRIP, :] = strip[:, lanes:]
        if top + STRIP < wide:
            above = (top + STRIP) // lanes * lanes
            below = strip[:, above - low * lanes:wide - low * lanes]
            work[above:, live] -= product(below, strip, (0, 0))
        yield


def reduce_kernel(sums_ref, inverse, panels, c_ref, reduced, top_rows, high, low, forward, backward):
    blk = c_ref.shape[2]
    step = pl.program_id(0)

    @pl.when(step == 0)
    def _():
        forward[0], forward[1] = split(inverse[...])
        backward[0], backward[1] = split(inverse[...].T)
        high[...], low[...] = split(jnp.concatenate([panels[0], panels[1]], axis=1))

    cross = jnp.concatenate([sums_ref[2 * step], sums_ref[2 * step + 1]], axis=1)
    weights = split_product((forward[0], forward[1]), split(cross))
    top_rows[0] = weights[:, :blk]
    top_rows[1] = weights[:, blk:]
    coefficients = split_product((backward[0], backward[1]), split(weights))
    span = split_product((high[...], low[...]), split(coefficients))
    reduced[0] = c_ref[0] - span[:, :blk]
    reduced[1] = c_ref[1] - span[:, blk:]


def reduce(total, inverse, panels, block):
    rounds, rows_dev, blk = block.shape
    wide = 2 * blk
    shape = jax.ShapeDtypeStruct
    whole = lambda array: pl.BlockSpec(array.shape, lambda i: (0,) * len(array.shape))
    pair = pl.BlockSpec((2, rows_dev, blk), lambda i: (i, 0, 0))
    return pl.pallas_call(
        reduce_kernel,
        grid=(rounds // 2,),
        out_shape=(shape(block.shape, jnp.float32), shape((rounds, wide, blk), jnp.float32)),
        in_specs=[whole(total), whole(inverse), whole(panels), pair],
        out_specs=(pair, pl.BlockSpec((2, wide, blk), lambda i: (i, 0, 0))),
        scratch_shapes=[pltpu.VMEM((rows_dev, wide), jnp.bfloat16)] * 2 + [pltpu.VMEM((2, wide, wide), jnp.bfloat16)] * 2,
        compiler_params=pltpu.CompilerParams(vmem_limit_bytes=48 * 2**20),
        name="reduce_columns",
    )(total, inverse, panels, block)


def solution(mesh):
    n, chips = mesh.shape["rows"], mesh.shape["cols"] // 2

    def shards(matrix):
        block = jnp.transpose(matrix, (1, 0, 2))
        panels, total, inverse = sums(block, n, chips)
        reduced, top_rows = reduce(total, inverse, panels, block)
        return jnp.transpose(reduced, (1, 0, 2)), jnp.transpose(top_rows, (1, 0, 2))

    return jax.shard_map(
        shards,
        mesh=mesh,
        in_specs=(P("rows", None, "cols"),),
        out_specs=(P("rows", None, "cols"), P(None, None, "cols")),
        check_vma=False,
    )
```
